128 devices in a mesh: dp: 16 (over y, x), mp: 8 (over z, core).
Axes of the slice: x: 4, y: 4, z: 4, core: 2. Of those that a mesh axis runs over, the one named last changes fastest.
Arguments:
- tokens: bfloat16 [16384, 5120], P('dp'), may hold values from -6 to 6
- norm_gain: bfloat16 [5120], replicated, may hold values from 0.099609375 to 1.8984375
- w_query: bfloat16 [5120, 5120], P('dp', 'mp'), may hold values from -0.078125 to 0.078125
- b_query: bfloat16 [5120], P('mp'), may hold values from -3 to 3
- keyvalue_weight: bfloat16 [5120, 2, 1024], P('dp', None, 'mp'), may hold values from -0.078125 to 0.078125
- b_keyval: bfloat16 [2, 1024], P(None, 'mp'), may hold values from -3 to 3
- w_out: bfloat16 [5120, 5120], P('mp', 'dp'), may hold values from -0.5 to 0.5
- kv_pool: bfloat16 [2, 1024, 64, 1024], P(None, 'dp', None, 'mp'), may hold values from -64 to 64
- page_owner: int32 [16, 16], replicated, may hold values from 0 to 15, as said below
- page_index: int32 [16, 16], replicated, may hold values from 0 to 63
- prefix_pages: int32 [16], replicated, may hold values from 10 to 16, as said below
- prompt_device: int32 [16], replicated, may hold values from 0 to 15, each once
Outputs:
- attn_out: bfloat16 [16384, 5120], P('dp', 'mp')
The draws below stay inside these ranges and needn't reach their ends.
Inputs may be any that keep to these rules, and one draw needn't show every extreme that they name: `page_owner`: slots at or beyond a prompt's prefix_pages are unused. Of one prompt's used slots at most 2 name the same owner, and some prompt has exactly 2 used slots with one owner. `prefix_pages`: some prompt has 16 used slots.
All inputs are finite; a program needn't handle non-finite values.
Results may differ from the reference program's by a relative error of at most 0.014.
The reference program's roundings to bfloat16 on the way count: a program that leaves them out, or rounds other values in their place, can miss the bound.
Values may be sent and summed in bfloat16 or wider, within the bound.
No kernel may reach another device: no remote copies, remote signals or barrier semaphores. Data moves between devices by JAX's collectives and lax.ppermute only.
A program may use at most 192 MiB of HBM per device.

```python
import jax
import jax.numpy as jnp
from jax import lax

D = 5120
H = 40
KVH = 8
HD = 128
SUFFIX = 1024
PAGE = 64
MAXP = 16
CAP = 2
POOL = 64
TOKENS = 16384
N_DP = 16
N_MP = 8


def page_plan(key):
    base = jax.random.fold_in(key, 7)
    key_len, key_top, key_rating, key_frequent, key_index = jax.random.split(base, 5)
    lengths = jax.random.randint(key_len, (N_DP,), MAXP - 3 * MAXP // 8, MAXP + 1)
    longest = jax.random.randint(key_top, (), 0, N_DP)
    lengths = jnp.where(jnp.arange(N_DP) == longest, MAXP, lengths).astype(jnp.int32)
    frequent_ranking = jax.random.permutation(key_frequent, N_DP)
    frequent_count = max(1, N_DP // 4)
    score_extra = jnp.where(frequent_ranking < frequent_count, 512, 0)
    logit_scores = jax.random.randint(key_rating, (N_DP, N_DP), 0, 1024) - score_extra[None, :]
    distinct = logit_scores * N_DP + jnp.arange(N_DP)[None, :]
    owner_list = jnp.argsort(distinct, axis=1, stable=True)
    slot_run = jnp.broadcast_to((jnp.arange(MAXP) // CAP)[None, :], (N_DP, MAXP))
    owners = jnp.take_along_axis(owner_list, slot_run, axis=1).astype(jnp.int32)
    indices = jax.random.randint(key_index, (N_DP, MAXP), 0, POOL).astype(jnp.int32)
    return (owners, indices, lengths)


def draw_page_owner(key, part):
    return page_plan(key)[0]


def draw_page_index(key, part):
    return page_plan(key)[1]


def draw_prefix_pages(key, part):
    return page_plan(key)[2]


def draw_kv_pool(key, part):
    key_main = jax.random.fold_in(jax.random.fold_in(key, 11), 0)
    shape = (2, N_DP * POOL, PAGE, KVH * HD)
    values = jnp.clip(jax.random.normal(key_main, shape, jnp.float32), -6.0, 6.0)
    return values.astype(jnp.bfloat16)


def block_scale(key, extent, cuts, smallest, top_value):
    def one(position, shards_of):
        heights = jax.random.uniform(jax.random.fold_in(jax.random.fold_in(key, 6), position), (shards_of,), jnp.float32, smallest / len(cuts), top_value / len(cuts))
        return jnp.repeat(jnp.exp(heights), extent[position] // shards_of).reshape((-1,) + (1,) * (len(extent) - position - 1))

    loudness = one(*cuts[0])
    for cut in cuts[1:]:
        loudness = loudness * one(*cut)
    return loudness


def bell_draw(rng, extent, scale, bound, cuts=(), held_as=jnp.bfloat16):
    drawn = scale * jax.random.normal(rng, extent, jnp.float32)
    if cuts:
        drawn = drawn * block_scale(rng, extent, cuts, -0.22, 0.18)
    return jnp.clip(drawn, -bound, bound).astype(held_as)


def setup_inputs(seed: int = 0) -> dict:
    splits = jax.random.split(jax.random.key(seed), 13)
    return {
        "tokens": bell_draw(splits[0], (TOKENS, D), 1.0, 6.0, ((0, 16),)),
        "norm_gain": jnp.clip(1.0 + 0.18 * jax.random.normal(splits[1], (D,), jnp.float32), 0.099609375, 1.8984375).astype(jnp.bfloat16),
        "w_query": bell_draw(splits[2], (D, H * HD), D ** -0.5, 0.078125, ((0, 16), (1, 8))),
        "b_query": bell_draw(splits[3], (H * HD,), 0.5, 3.0, ((0, 8),)),
        "keyvalue_weight": bell_draw(splits[4], (D, 2, KVH * HD), D ** -0.5, 0.078125, ((0, 16), (2, 8))),
        "b_keyval": bell_draw(splits[5], (2, KVH * HD), 0.5, 3.0, ((1, 8),)),
        "w_out": bell_draw(splits[6], (H * HD, D), HD ** -0.5, 0.5, ((0, 8), (1, 16))),
        "kv_pool": draw_kv_pool(jax.random.fold_in(splits[12], 71), 0),
        "page_owner": draw_page_owner(jax.random.fold_in(splits[12], 71), 0),
        "page_index": draw_page_index(jax.random.fold_in(splits[12], 71), 0),
        "prefix_pages": draw_prefix_pages(jax.random.fold_in(splits[12], 71), 0),
        "prompt_device": jax.random.permutation(splits[11], N_DP).astype(jnp.int32),
    }


rope_theta = 1000000.0
norm_eps = 1e-06
masked_score = -1e+30

def rms_normed(rows, norm_gain):
    values = rows.astype(jnp.float32)
    inverse = lax.rsqrt(lax.optimization_barrier(jnp.mean(values * values, axis=-1, keepdims=True)) + norm_eps)
    return (values * inverse * norm_gain.astype(jnp.float32)).astype(jnp.bfloat16)

def rotary(values, positions):
    half_dim = values.shape[-1] // 2
    frequency = rope_theta ** (-jnp.arange(half_dim, dtype=jnp.float32) * 2.0 / values.shape[-1])
    angles = positions.astype(jnp.float32)[:, None] * frequency[None, :]
    cosine = jnp.cos(angles)[:, None, :]
    sine_part = jnp.sin(angles)[:, None, :]
    front_half = values[..., :half_dim]
    back_half = values[..., half_dim:]
    return jnp.concatenate([front_half * cosine - back_half * sine_part, back_half * cosine + front_half * sine_part], axis=-1)

def head_attention(query, keys, values, allowed):
    logit_scores = jnp.einsum('sgd,nd->gsn', query.astype(jnp.float32), keys.astype(jnp.float32)) * HD ** (-0.5)
    logit_scores = jnp.where(allowed[None], logit_scores, masked_score)
    top = lax.optimization_barrier(jnp.max(logit_scores, axis=-1, keepdims=True))
    raised = jnp.exp(logit_scores - top)
    weights = (raised / lax.optimization_barrier(jnp.sum(raised, axis=-1, keepdims=True))).astype(jnp.bfloat16)
    return jnp.einsum('gsn,nd->sgd', weights.astype(jnp.float32), values.astype(jnp.float32)).astype(jnp.bfloat16)

def reference(tokens, norm_gain, w_query, b_query, keyvalue_weight, b_keyval, w_out, kv_pool, page_owner, page_index, prefix_pages, prompt_device):
    slot_prompt = jnp.zeros((N_DP,), jnp.int32).at[prompt_device].set(jnp.arange(N_DP, dtype=jnp.int32))
    token_blocks = tokens.reshape(N_DP, SUFFIX, D)
    flat_keyval = keyvalue_weight.reshape(D, 2 * KVH * HD)

    def one_group(item):
        rows, prompt = item
        normed = rms_normed(rows, norm_gain)
        query = jnp.dot(normed, w_query, preferred_element_type=jnp.float32) + b_query.astype(jnp.float32)
        keyval = jnp.dot(normed, flat_keyval, preferred_element_type=jnp.float32) + b_keyval.reshape(2 * KVH * HD).astype(jnp.float32)
        length = prefix_pages[prompt]
        positions = length * PAGE + jnp.arange(SUFFIX, dtype=jnp.int32)
        rotated = rotary(query.reshape(SUFFIX, H, HD), positions).astype(jnp.bfloat16)
        new_keys = rotary(keyval[:, :KVH * HD].reshape(SUFFIX, KVH, HD), positions).astype(jnp.bfloat16)
        new_values = keyval[:, KVH * HD:].reshape(SUFFIX, KVH, HD).astype(jnp.bfloat16)
        flat_pages = (page_owner[prompt] * POOL + page_index[prompt]).astype(jnp.int32)
        cached = jnp.take(kv_pool, flat_pages, axis=1).reshape(2, MAXP * PAGE, KVH, HD)
        keys = jnp.concatenate([cached[0], new_keys], axis=0)
        values = jnp.concatenate([cached[1], new_values], axis=0)
        page_live = jnp.arange(MAXP * PAGE, dtype=jnp.int32) < length * PAGE
        token_ids = jnp.arange(SUFFIX, dtype=jnp.int32)
        causal = token_ids[None, :] <= token_ids[:, None]
        allowed = jnp.concatenate([jnp.broadcast_to(page_live[None, :], (SUFFIX, MAXP * PAGE)), causal], axis=1)
        grouped = rotated.reshape(SUFFIX, KVH, H // KVH, HD).transpose(1, 0, 2, 3)
        heads_out = lax.map(lambda part: head_attention(part[0], part[1], part[2], allowed), (grouped, keys.transpose(1, 0, 2), values.transpose(1, 0, 2)))
        attended = heads_out.transpose(1, 0, 2, 3).reshape(SUFFIX, H * HD)
        per_shard = attended.reshape(SUFFIX, N_MP, H * HD // N_MP)
        out_rows = w_out.reshape(N_MP, H * HD // N_MP, D)
        total = jnp.zeros((SUFFIX, D), jnp.float32)
        for shard in range(N_MP):
            term = jnp.dot(per_shard[:, shard], out_rows[shard], preferred_element_type=jnp.float32)
            total = total + lax.optimization_barrier(term.astype(jnp.bfloat16)).astype(jnp.float32)
        return total.astype(jnp.bfloat16)
    result = lax.map(one_group, (token_blocks, slot_prompt))
    return result.reshape(N_DP * SUFFIX, D)
```

```python
import functools

import jax
import jax.numpy as jnp
from jax import lax
from jax.experimental import pallas as pl
from jax.experimental.pallas import tpu as pltpu
from jax.sharding import PartitionSpec as P

HD = 128
CAP = 2
SIDE = 4
ROWS = 256
VMEM_LIMIT = 56 * 2**20

rope_theta = 1000000.0
norm_eps = 1e-06
masked_score = -1e30

SHIFTS = (0, 1, 3, 2)


def rms_normed(rows, norm_gain):
    values = rows.astype(jnp.float32)
    inverse = lax.rsqrt(jnp.mean(values * values, axis=-1, keepdims=True) + norm_eps)
    return (values * inverse * norm_gain.astype(jnp.float32)).astype(jnp.bfloat16)


def shift_plane(block, d, turn):
    if d == 0:
        return block
    pairs = []
    for y in range(SIDE):
        for x in range(SIDE):
            for member in range(2 * SIDE):
                if member % 2 == turn:
                    target = y * SIDE + (x + d) % SIDE
                else:
                    target = (y + d) % SIDE * SIDE + x
                pairs.append(((y * SIDE + x) * 2 * SIDE + member, target * 2 * SIDE + member))
    return lax.ppermute(block, ("dp", "mp"), pairs)


def shift_z(block, d):
    pairs = [(z * 2 + c, (z + d) % SIDE * 2 + c) for z in range(SIDE) for c in range(2)]
    return block if d == 0 else lax.ppermute(block, "mp", pairs)


def swap_core(block):
    return lax.ppermute(block, "mp", [(m, m ^ 1) for m in range(2 * SIDE)])


def to_own_plane(block):
    pairs = []
    for y in range(SIDE):
        for x in range(SIDE):
            for z in range(SIDE):
                for c in range(2):
                    source = (y * SIDE + x) * 8 + z * 2 + c
                    target = (z * SIDE + 2 * (x % 2) + c) * 8 + y * 2 + x // 2
                    pairs.append((source, target))
    return lax.ppermute(block, ("dp", "mp"), pairs)


def send_pages_kernel(pick_ref, device_ref, pool, out, sems):
    prompts = device_ref.shape[0]
    copies = [
        pltpu.make_async_copy(
            pool.at[:, pick_ref[p * CAP + r]], out.at[device_ref[p], r], sems.at[p * CAP + r]
        )
        for p in range(prompts)
        for r in range(CAP)
    ]
    for copy in copies:
        copy.start()
    for copy in copies:
        copy.wait()


def send_pages(my_group, page_owner, page_index, prefix_pages, prompt_device, kv_pool):
    prompts, slots = page_owner.shape
    _, held, page_len, width = kv_pool.shape
    slot = jnp.arange(slots, dtype=jnp.int32)[None, :]
    mine = (slot < prefix_pages[:, None]) & (page_owner == my_group)
    keyed = slot * held + page_index
    first = jnp.min(jnp.where(mine, keyed, slots * held), axis=1) % held
    final = jnp.max(jnp.where(mine, keyed, 0), axis=1) % held
    pick = jnp.stack([first, final], axis=1).reshape(-1)
    smem = pl.BlockSpec(memory_space=pltpu.SMEM)
    return pl.pallas_call(
        send_pages_kernel,
        out_shape=jax.ShapeDtypeStruct((prompts, CAP, 2, page_len, width), kv_pool.dtype),
        in_specs=[smem] * 2 + [pl.BlockSpec(memory_space=pl.ANY)],
        out_specs=pl.BlockSpec(memory_space=pltpu.VMEM),
        scratch_shapes=[pltpu.SemaphoreType.DMA((prompts * CAP,))],
    )(pick, prompt_device, kv_pool)


def weight_copies(chunk, layout, me, core, target, sems):
    x, y = me % SIDE, me // SIDE
    copies = []
    for ref, (at, outer, lane, width) in zip(chunk, layout):
        block = ref.shape[0] // SIDE
        for b, inner in enumerate(SHIFTS):
            dx = inner + core * (outer - inner)
            dy = outer + core * (inner - outer)
            source = (y + SIDE - dy) % SIDE * SIDE + (x + SIDE - dx) % SIDE
            copies.append(
                pltpu.make_async_copy(
                    ref.at[pl.ds(b * block, block), pl.ds(at, width)],
                    target(source, lane, width),
                    sems.at[len(copies)],
                )
            )
    return copies


def attention_kernel(heads, first, layout, *refs):
    refs = list(refs)
    me_ref = refs.pop(0)
    if first:
        place_ref = refs.pop(0)
    normed_ref = refs.pop(0)
    chunk = [refs.pop(0) for _ in layout]
    bias_ref, cos_ref, sin_ref = refs.pop(0), refs.pop(0), refs.pop(0)
    if first:
        pages = refs.pop(0)
        out_ref, keys_ref, values_ref = refs.pop(0), refs.pop(0), refs.pop(0)
        weights, weight_sems, page_sems = refs
    else:
        keys_ref, values_ref = refs.pop(0), refs.pop(0)
        out_ref = refs.pop(0)
        weights, weight_sems = refs
    step = pl.program_id(0)
    me, core, length = me_ref[0], me_ref[1] % 2, me_ref[2]
    local = weights.shape[0] // (SIDE * SIDE)
    page_len = 64
    cached = keys_ref.shape[0] - ROWS * SIDE
    slots = cached // page_len

    @pl.when(step == 0)
    def _():
        def target(source, lane, width):
            row = pl.multiple_of(source * local, 16)
            return weights.at[pl.ds(row, local), pl.ds(lane, width)]

        copies = weight_copies(chunk, layout, me, core, target, weight_sems)
        if first:
            for j in range(slots):
                for part, held in ((0, keys_ref), (1, values_ref)):
                    copies.append(
                        pltpu.make_async_copy(
                            pages.at[place_ref[j], part],
                            held.at[pl.ds(j * page_len, page_len)],
                            page_sems.at[j * 2 + part],
                        )
                    )
        for copy in copies:
            copy.start()
        for copy in copies:
            copy.wait()

    projected = (
        jnp.dot(normed_ref[...], weights[...], preferred_element_type=jnp.float32) + bias_ref[...]
    )
    cosine, sine = cos_ref[...], sin_ref[...]

    def rotated(column):
        vector = projected[:, column : column + HD]
        return (vector * cosine + pltpu.roll(vector, HD // 2, 1) * sine).astype(jnp.bfloat16)

    column = 0
    if first:
        row = pl.multiple_of(cached + step * ROWS, ROWS)
        keys_ref[pl.ds(row, ROWS), :] = rotated(0)
        values_ref[pl.ds(row, ROWS), :] = projected[:, HD : 2 * HD].astype(jnp.bfloat16)
        column = 2 * HD
    query = jnp.concatenate([rotated(column + h * HD) for h in range(heads)], axis=0)
    to_exponent = HD ** (-0.5) * 1.4426950408889634

    def product(part):
        return lax.dot_general(
            query, part, (((1,), (1,)), ((), ())), preferred_element_type=jnp.float32
        )

    for now in range(SIDE):

        @pl.when(step == now)
        def _(now=now):
            whole = cached + now * ROWS
            live = lax.broadcasted_iota(jnp.int32, (1, cached), 1) < length * page_len
            scores = [jnp.where(live, product(keys_ref[0:cached, :]), masked_score)]
            if now:
                scores.append(product(keys_ref[cached:whole, :]))
            row_ids = lax.broadcasted_iota(jnp.int32, (ROWS, ROWS), 0)
            column_ids = lax.broadcasted_iota(jnp.int32, (ROWS, ROWS), 1)
            causal = jnp.concatenate([column_ids <= row_ids] * heads, axis=0)
            scores.append(
                jnp.where(causal, product(keys_ref[whole : whole + ROWS, :]), masked_score)
            )
            top = functools.reduce(
                jnp.maximum, [jnp.max(s, axis=-1, keepdims=True) for s in scores]
            )
            raised = [jnp.exp2((s - top) * to_exponent) for s in scores]
            total = sum(jnp.sum(r, axis=-1, keepdims=True) for r in raised)
            spots = [(0, cached), (cached, whole), (whole, whole + ROWS)]
            if not now:
                spots.pop(1)
            mixed = sum(
                jnp.dot(
                    r.astype(jnp.bfloat16),
                    values_ref[begin:end, :],
                    preferred_element_type=jnp.float32,
                )
                for r, (begin, end) in zip(raised, spots)
            )
            mixed = (mixed / total).astype(jnp.bfloat16)
            for h in range(heads):
                out_ref[h] = mixed[h * ROWS : (h + 1) * ROWS]


def attention(me, normed, chunk, bias, cosine, sine, heads, place=None, pages=None, cache=None):
    first = cache is None
    rows, depth = normed.shape
    columns = bias.shape[1]
    layout = tuple(part[1:] for part in chunk)
    pieces = [part[0] for part in chunk]
    smem = pl.BlockSpec(memory_space=pltpu.SMEM)
    anywhere = pl.BlockSpec(memory_space=pl.ANY)
    by_rows = pl.BlockSpec((ROWS, HD), lambda i: (i, 0))
    slots = place.shape[0] if first else 0
    total = rows + slots * 64 if first else cache[0].shape[0]
    whole = pl.BlockSpec((total, HD), lambda i: (0, 0))
    operands, in_specs = [me], [smem]
    if first:
        operands.append(place)
        in_specs.append(smem)
    operands += [normed, *pieces, bias, cosine, sine]
    in_specs += [pl.BlockSpec((ROWS, depth), lambda i: (i, 0))] + [anywhere] * len(pieces)
    in_specs += [pl.BlockSpec((1, columns), lambda i: (0, 0)), by_rows, by_rows]
    out_shape = [jax.ShapeDtypeStruct((heads, rows, HD), jnp.bfloat16)]
    out_specs = [pl.BlockSpec((heads, ROWS, HD), lambda i: (0, i, 0))]
    scratch = [
        pltpu.VMEM((depth, columns), jnp.bfloat16),
        pltpu.SemaphoreType.DMA((len(pieces) * SIDE,)),
    ]
    if first:
        operands.append(pages)
        in_specs.append(anywhere)
        out_shape += [jax.ShapeDtypeStruct((total, HD), jnp.bfloat16)] * 2
        out_specs += [whole, whole]
        scratch.append(pltpu.SemaphoreType.DMA((2 * slots,)))
    else:
        operands += list(cache)
        in_specs += [whole, whole]
    return pl.pallas_call(
        functools.partial(attention_kernel, heads, first, layout),
        grid=(rows // ROWS,),
        out_shape=out_shape,
        in_specs=in_specs,
        out_specs=out_specs,
        scratch_shapes=scratch,
        compiler_params=pltpu.CompilerParams(vmem_limit_bytes=VMEM_LIMIT),
        cost_estimate=pl.CostEstimate(
            flops=2 * rows * depth * columns + 4 * rows * total * HD * heads,
            bytes_accessed=2 * depth * (rows + columns),
            transcendentals=rows * total * heads,
        ),
    )(*operands)


def output_kernel(width, last, layout, spots, *refs):
    refs = list(refs)
    place_ref = refs.pop(0)
    before = refs.pop(0) if last else None
    blocks = [refs.pop(0) for _ in spots]
    chunk = [refs.pop(0) for _ in layout]
    out_ref = refs.pop(0)
    left, right, left_sems, right_sems = refs
    me, member = place_ref[0], place_ref[1]
    z, c = member // 2, member % 2
    local = right.shape[0] // 2
    rows = left.shape[0]

    def target(source, lane, wide):
        group = source // SIDE * 2 + source % 2
        row = pl.multiple_of(source % SIDE // 2 * local, 16)
        column = pl.multiple_of(group * width + lane, HD)
        return right.at[pl.ds(row, local), pl.ds(column, wide)]

    copies = weight_copies(chunk, layout, me, c, target, right_sems)
    k = 0
    for ref, (swapped, parts) in zip(blocks, spots):
        for at, shift, head, row, count in parts:
            group = (z + SIDE - shift) % SIDE * 2 + (1 - c if swapped else c)
            column = pl.multiple_of(group * width + head * HD, HD)
            copies.append(
                pltpu.make_async_copy(
                    ref.at[pl.ds(at, count)],
                    left.at[pl.ds(row, count), pl.ds(column, HD)],
                    left_sems.at[k],
                )
            )
            k += 1
    for copy in copies:
        copy.start()
    for copy in copies:
        copy.wait()
    for begin in range(0, rows, ROWS):
        total = lax.dot_general(
            left[begin : begin + ROWS, :],
            right[...],
            (((1,), (1,)), ((), ())),
            preferred_element_type=jnp.float32,
        )
        if last:
            total = total + before[begin : begin + ROWS, :]
        out_ref[begin : begin + ROWS, :] = total.astype(out_ref.dtype)


def output_part(place, rows, heads, blocks, chunk, columns, before=None):
    last = before is not None
    width = heads * HD
    layout = tuple(part[1:] for part in chunk)
    pieces = [part[0] for part in chunk]
    spots = tuple(spot for _, spot in blocks)
    blocks = [block for block, _ in blocks]
    strips = sum(len(parts) for _, parts in spots)
    anywhere = pl.BlockSpec(memory_space=pl.ANY)
    vmem = pl.BlockSpec(memory_space=pltpu.VMEM)
    operands, in_specs = [place], [pl.BlockSpec(memory_space=pltpu.SMEM)]
    if last:
        operands.append(before)
        in_specs.append(vmem)
    operands += [*blocks, *pieces]
    in_specs += [anywhere] * (len(blocks) + len(pieces))
    return pl.pallas_call(
        functools.partial(output_kernel, width, last, layout, spots),
        out_shape=jax.ShapeDtypeStruct((rows, columns), jnp.bfloat16 if last else jnp.float32),
        in_specs=in_specs,
        out_specs=vmem,
        scratch_shapes=[
            pltpu.VMEM((rows, 2 * SIDE * width), jnp.bfloat16),
            pltpu.VMEM((columns, 2 * SIDE * width), jnp.bfloat16),
            pltpu.SemaphoreType.DMA((strips,)),
            pltpu.SemaphoreType.DMA((len(pieces) * SIDE,)),
        ],
        compiler_params=pltpu.CompilerParams(vmem_limit_bytes=VMEM_LIMIT),
        cost_estimate=pl.CostEstimate(
            flops=4 * SIDE * rows * columns * width,
            bytes_accessed=4 * SIDE * width * (rows + columns),
            transcendentals=0,
        ),
    )(*operands)


def shards(
    tokens,
    norm_gain,
    w_query,
    b_query,
    keyvalue_weight,
    b_keyval,
    w_out,
    kv_pool,
    page_owner,
    page_index,
    prefix_pages,
    prompt_device,
):
    my_group = lax.axis_index("dp")
    my_member = lax.axis_index("mp")
    rows = tokens.shape[0]
    local, width_kv = keyvalue_weight.shape[0], keyvalue_weight.shape[2]
    page_len = kv_pool.shape[2]

    packed = jnp.concatenate([keyvalue_weight.reshape(local, 2 * width_kv), w_query], axis=1)
    along = [shift_plane(packed, d, 0) for d in SHIFTS]

    moved = to_own_plane(w_out.T)
    length = jnp.sum(jnp.where(prompt_device == my_group, prefix_pages, 0))
    outgoing = send_pages(
        my_group, page_owner, page_index, prefix_pages, prompt_device, kv_pool
    )
    arrived = lax.all_to_all(outgoing, "dp", split_axis=0, concat_axis=0)
    pages = arrived.reshape((-1,) + arrived.shape[2:])
    owners = jnp.sum(jnp.where((prompt_device == my_group)[:, None], page_owner, 0), axis=0)
    slot = jnp.arange(owners.shape[0], dtype=jnp.int32)
    again = jnp.any((owners[:, None] == owners[None, :]) & (slot[None, :] < slot[:, None]), axis=1)
    slot_place = jnp.where(slot < length, owners * CAP + again, owners[0] * CAP).astype(jnp.int32)

    normed = rms_normed(tokens, norm_gain)
    positions = (length * page_len + jnp.arange(rows, dtype=jnp.int32)).astype(jnp.float32)
    frequency = rope_theta ** (-jnp.arange(HD // 2, dtype=jnp.float32) * 2.0 / HD)
    angles = positions[:, None] * frequency[None, :]
    cosine, sine = jnp.cos(angles), jnp.sin(angles)
    cosine = jnp.concatenate([cosine, cosine], axis=1)
    sine = jnp.concatenate([-sine, sine], axis=1)
    bias = jnp.concatenate([b_keyval.reshape(-1), b_query]).astype(jnp.float32)[None, :]
    me = jnp.stack([my_group, my_member, length]).astype(jnp.int32)
    place = jnp.stack([my_group, my_member]).astype(jnp.int32)

    columns = w_out.shape[0]
    spans = ((0, 1), (1, 2), (3, 2))
    edges = [(0, 3 * HD), (3 * HD, 5 * HD), (5 * HD, 7 * HD)]
    splits = [2 * HD, HD, HD, 3 * HD]
    stacks = [
        jnp.concatenate([piece[:, begin:end] for piece in along], axis=0) for begin, end in edges
    ]
    stacks.append(jnp.concatenate([shift_plane(moved, d, 0) for d in SHIFTS], axis=0))
    chunks, ahead, behind = [], None, None
    for k, stack in enumerate(stacks):
        wide = stack.shape[1]
        up, down = stack, stack
        if k:
            split, before = splits[k - 1], stacks[k - 1].shape[1]
            up = jnp.concatenate([stack, ahead[:, :split]], axis=1)
            down = jnp.concatenate([stack, behind[:, split:before]], axis=1)
        ahead, behind = shift_plane(up, 1, 1), shift_plane(down, 3, 1)
        if k:
            chunks[-1] += [(ahead, wide, 2, 0, split), (behind, wide, 2, split, before - split)]
        chunks.append([(stack, 0, 0, 0, wide), (ahead, 0, 1, 0, wide), (behind, 0, 3, 0, wide)])
    split = splits[-1]
    chunks[-1] += [
        (shift_plane(ahead[:, :split], 1, 1), 0, 2, 0, split),
        (shift_plane(behind[:, split:wide], 3, 1), 0, 2, split, wide - split),
    ]

    cache, blocks, ahead, behind = None, [], None, None
    sent = []
    for (head, count), (begin, end), chunk in zip(spans, edges, chunks):
        part = functools.partial(
            attention, me, normed, chunk, bias[:, begin:end], cosine, sine, count
        )
        if cache is None:
            attended, *cache = part(place=slot_place, pages=pages)
        else:
            (attended,) = part(cache=cache)
        sent.append(attended.reshape(count * rows, HD))

    def strips(at, shift, head, begin, count):
        parts = []
        while count:
            row = begin % rows
            step = min(count, rows - row)
            parts.append((at, shift, head + begin // rows, row, step))
            at, begin, count = at + step, begin + step, count - step
        return parts

    held = []
    for k in range(len(sent) + 1):
        ups, downs, up_parts, down_parts = [], [], [], []
        if k < len(sent):
            head, size = spans[k][0], sent[k].shape[0]
            held.append((sent[k], {k: strips(0, 0, head, 0, size)}))
            ups, downs = [sent[k]], [sent[k]]
            up_parts = [(k, strips(0, 1, head, 0, size))]
            down_parts = [(k, strips(0, 3, head, 0, size))]
        if k:
            at = sent[k].shape[0] if k < len(sent) else 0
            head, size = spans[k - 1][0], sent[k - 1].shape[0]
            ups.append(ahead[: size // 2])
            downs.append(behind[size // 2 : size])
            up_parts.append((k - 1, strips(at, 2, head, 0, size // 2)))
            down_parts.append((k - 1, strips(at, 2, head, size // 2, size // 2)))
        ahead = shift_z(jnp.concatenate(ups, axis=0), 1)
        behind = shift_z(jnp.concatenate(downs, axis=0), 3)
        held += [(ahead, dict(up_parts)), (behind, dict(down_parts))]
    held = [(array, parts, False) for array, parts in held] + [
        (swap_core(array), parts, True) for array, parts in held
    ]

    def heads_of(some):
        first = spans[some[0]][0]
        found = []
        for array, parts, swapped in held:
            here = tuple(
                (at, shift, head - first, row, count)
                for k in some
                for at, shift, head, row, count in parts.get(k, ())
            )
            if here:
                found.append((array, (swapped, here)))
        return found

    def lanes(begin, end):
        return [
            (ref, at + max(begin - lane, 0), shift, max(lane - begin, 0), min(end, lane + wide) - max(begin, lane))
            for ref, at, shift, lane, wide in chunks[-1]
            if lane < end and lane + wide > begin
        ]

    cut = spans[2][0]
    total = columns // HD
    early = output_part(place, rows, cut, heads_of((0, 1)), lanes(0, cut * HD), columns)
    return output_part(
        place, rows, total - cut, heads_of((2,)), lanes(cut * HD, columns), columns, before=early
    )


def solution(mesh):
    return jax.shard_map(
        shards,
        mesh=mesh,
        in_specs=(
            P("dp", None),
            P(),
            P("dp", "mp"),
            P("mp"),
            P("dp", None, "mp"),
            P(None, "mp"),
            P("mp", "dp"),
            P(None, "dp", None, "mp"),
            P(),
            P(),
            P(),
            P(),
        ),
        out_specs=P("dp", "mp"),
        check_vma=False,
    )
```

```python
import functools

import jax
import jax.numpy as jnp
from jax import lax
from jax.experimental import pallas as pl
from jax.experimental.pallas import tpu as pltpu
from jax.sharding import PartitionSpec as P

HD = 128
CAP = 2
SIDE = 4
ROWS = 256
STEPS = 4
VMEM_LIMIT = 56 * 2**20
SLIGHT = pl.CostEstimate(flops=1, bytes_accessed=1, transcendentals=0)

rope_theta = 1000000.0
norm_eps = 1e-06
masked_score = -1e30

SHIFTS = (0, 1, 3, 2)


def rms_normed(rows, norm_gain):
    values = rows.astype(jnp.float32)
    inverse = lax.rsqrt(jnp.mean(values * values, axis=-1, keepdims=True) + norm_eps)
    return (values * inverse * norm_gain.astype(jnp.float32)).astype(jnp.bfloat16)


def shift_plane(block, d, turn):
    if d == 0:
        return block
    pairs = []
    for y in range(SIDE):
        for x in range(SIDE):
            for member in range(2 * SIDE):
                if member % 2 == turn:
                    target = y * SIDE + (x + d) % SIDE
                else:
                    target = (y + d) % SIDE * SIDE + x
                pairs.append(((y * SIDE + x) * 2 * SIDE + member, target * 2 * SIDE + member))
    return lax.ppermute(block, ("dp", "mp"), pairs)


def one_turn(block, turn, before_rest=None):
    half = block.shape[0] // 2
    ahead, behind = shift_plane(block, 1, turn), shift_plane(block, 3, turn)
    if before_rest is not None:
        ahead, behind, _ = lax.optimization_barrier((ahead, behind, before_rest))
    far = (shift_plane(ahead[:half], 1, turn), shift_plane(behind[half:], 3, turn))
    return ahead, behind, far


def ring_copies(pieces, layout, me, core, target, sems):
    x, y = me % SIDE, me // SIDE
    copies = []
    for ref, (outer, begin, count) in zip(pieces, layout):
        block = ref.shape[0] // count
        for i in range(count):
            inner = begin + i
            dx = inner + core * (outer - inner)
            dy = outer + core * (inner - outer)
            lane, width, place = target((x + SIDE - dx) % SIDE, (y + SIDE - dy) % SIDE)
            copies.append(
                pltpu.make_async_copy(
                    ref.at[pl.ds(i * block, block), pl.ds(lane, width)],
                    place,
                    sems.at[len(copies)],
                )
            )
    return copies


def shift_z(block, d):
    pairs = [(z * 2 + c, (z + d) % SIDE * 2 + c) for z in range(SIDE) for c in range(2)]
    return block if d == 0 else lax.ppermute(block, "mp", pairs)


def swap_core(block):
    return lax.ppermute(block, "mp", [(m, m ^ 1) for m in range(2 * SIDE)])


def to_own_plane(block):
    pairs = []
    for y in range(SIDE):
        for x in range(SIDE):
            for z in range(SIDE):
                for c in range(2):
                    source = (y * SIDE + x) * 8 + z * 2 + c
                    target = (z * SIDE + 2 * (x % 2) + c) * 8 + y * 2 + x // 2
                    pairs.append((source, target))
    return lax.ppermute(block, ("dp", "mp"), pairs)


def send_pages_kernel(pick_ref, device_ref, pool, out, sems):
    prompts = device_ref.shape[0]
    copies = [
        pltpu.make_async_copy(
            pool.at[:, pick_ref[p * CAP + r]], out.at[device_ref[p], r], sems.at[p * CAP + r]
        )
        for p in range(prompts)
        for r in range(CAP)
    ]
    for copy in copies:
        copy.start()
    for copy in copies:
        copy.wait()


def send_pages(my_group, page_owner, page_index, prefix_pages, prompt_device, kv_pool):
    prompts, slots = page_owner.shape
    _, held, page_len, width = kv_pool.shape
    slot = jnp.arange(slots, dtype=jnp.int32)[None, :]
    mine = (slot < prefix_pages[:, None]) & (page_owner == my_group)
    keyed = slot * held + page_index
    first = jnp.min(jnp.where(mine, keyed, slots * held), axis=1) % held
    final = jnp.max(jnp.where(mine, keyed, 0), axis=1) % held
    pick = jnp.stack([first, final], axis=1).reshape(-1)
    smem = pl.BlockSpec(memory_space=pltpu.SMEM)
    return pl.pallas_call(
        send_pages_kernel,
        out_shape=jax.ShapeDtypeStruct((prompts, CAP, 2, page_len, width), kv_pool.dtype),
        in_specs=[smem] * 2 + [pl.BlockSpec(memory_space=pl.ANY)],
        out_specs=pl.BlockSpec(memory_space=pltpu.VMEM),
        scratch_shapes=[pltpu.SemaphoreType.DMA((prompts * CAP,))],
    )(pick, prompt_device, kv_pool)


def projection_kernel(layout, place_ref, me_ref, normed_ref, bias_ref, cos_ref, sin_ref, pages, *refs):
    pieces, refs = refs[: len(layout)], refs[len(layout) :]
    query_ref, keys_ref, values_ref, weight_ref, weight_sems, page_sems = refs
    step = pl.program_id(0)
    slots = place_ref.shape[0]
    page_len = pages.shape[2]
    cached = slots * page_len

    local = weight_ref.shape[0] // (SIDE * SIDE)

    def target(x, y):
        row = pl.multiple_of((y * SIDE + x) * local, 16)
        return 0, weight_ref.shape[1], weight_ref.at[pl.ds(row, local)]

    weight_copies = ring_copies(pieces, layout, me_ref[0], me_ref[1] % 2, target, weight_sems)

    def page_copies():
        copies = []
        for j in range(slots):
            for part, held in ((0, keys_ref), (1, values_ref)):
                copies.append(
                    pltpu.make_async_copy(
                        pages.at[place_ref[j], part],
                        held.at[pl.ds(j * page_len, page_len)],
                        page_sems.at[j * 2 + part],
                    )
                )
        return copies

    @pl.when(step == 0)
    def _():
        for copy in weight_copies + page_copies():
            copy.start()
        for copy in weight_copies:
            copy.wait()

    cosine, sine = cos_ref[...], sin_ref[...]
    columns = weight_ref.shape[1]
    row = pl.multiple_of(cached + step * ROWS, ROWS)
    for begin in range(0, columns, 2 * HD):
        end = min(begin + 2 * HD, columns)
        projected = (
            jnp.dot(
                normed_ref[...], weight_ref[:, begin:end], preferred_element_type=jnp.float32
            )
            + bias_ref[:, begin:end]
        )
        for column in range(begin, end, HD):
            vector = projected[:, column - begin : column - begin + HD]
            if column == HD:
                values_ref[pl.ds(row, ROWS), :] = vector.astype(jnp.bfloat16)
                continue
            rotated = (vector * cosine + pltpu.roll(vector, HD // 2, 1) * sine).astype(jnp.bfloat16)
            if column == 0:
                keys_ref[pl.ds(row, ROWS), :] = rotated
            else:
                query_ref[column // HD - 2] = rotated

    @pl.when(step == pl.num_programs(0) - 1)
    def _():
        for copy in page_copies():
            copy.wait()


def projection(slot_place, me, normed, ring, bias, cosine, sine, pages):
    rows, depth = normed.shape
    columns = bias.shape[1]
    heads = columns // HD - 2
    slots, page_len = slot_place.shape[0], pages.shape[2]
    total = slots * page_len + rows
    smem = pl.BlockSpec(memory_space=pltpu.SMEM)
    anywhere = pl.BlockSpec(memory_space=pl.ANY)
    by_rows = pl.BlockSpec((ROWS, HD), lambda i: (i, 0))
    whole = pl.BlockSpec((total, HD), lambda i: (0, 0))
    return pl.pallas_call(
        functools.partial(projection_kernel, tuple(part[1:] for part in ring)),
        grid=(rows // ROWS,),
        out_shape=[
            jax.ShapeDtypeStruct((heads, rows, HD), jnp.bfloat16),
            jax.ShapeDtypeStruct((total, HD), jnp.bfloat16),
            jax.ShapeDtypeStruct((total, HD), jnp.bfloat16),
        ],
        in_specs=[
            smem,
            smem,
            pl.BlockSpec((ROWS, depth), lambda i: (i, 0)),
            pl.BlockSpec((1, columns), lambda i: (0, 0)),
            by_rows,
            by_rows,
            anywhere,
        ]
        + [anywhere] * len(ring),
        out_specs=[pl.BlockSpec((heads, ROWS, HD), lambda i: (0, i, 0)), whole, whole],
        scratch_shapes=[
            pltpu.VMEM((depth, columns), jnp.bfloat16),
            pltpu.SemaphoreType.DMA((SIDE * SIDE,)),
            pltpu.SemaphoreType.DMA((2 * slots,)),
        ],
        compiler_params=pltpu.CompilerParams(vmem_limit_bytes=VMEM_LIMIT),
        cost_estimate=SLIGHT,
    )(slot_place, me, normed, bias, cosine, sine, pages, *[part[0] for part in ring])


def attention_kernel(heads, page_len, length_ref, query_ref, keys_ref, values_ref, out_ref):
    step = pl.program_id(0)
    length = length_ref[0]
    cached = keys_ref.shape[0] - ROWS * STEPS
    query = query_ref[...].reshape(heads * ROWS, HD)
    to_exponent = HD ** (-0.5) * 1.4426950408889634

    def product(part):
        return lax.dot_general(
            query, part, (((1,), (1,)), ((), ())), preferred_element_type=jnp.float32
        )

    for now in range(STEPS):

        @pl.when(step == now)
        def _(now=now):
            whole = cached + now * ROWS
            live = lax.broadcasted_iota(jnp.int32, (1, cached), 1) < length * page_len
            scores = [jnp.where(live, product(keys_ref[0:cached, :]), masked_score)]
            if now:
                scores.append(product(keys_ref[cached:whole, :]))
            row_ids = lax.broadcasted_iota(jnp.int32, (ROWS, ROWS), 0)
            column_ids = lax.broadcasted_iota(jnp.int32, (ROWS, ROWS), 1)
            causal = jnp.concatenate([column_ids <= row_ids] * heads, axis=0)
            scores.append(
                jnp.where(causal, product(keys_ref[whole : whole + ROWS, :]), masked_score)
            )
            top = functools.reduce(
                jnp.maximum, [jnp.max(s, axis=-1, keepdims=True) for s in scores]
            )
            raised = [jnp.exp2((s - top) * to_exponent) for s in scores]
            total = sum(jnp.sum(r, axis=-1, keepdims=True) for r in raised)
            spots = [(0, cached), (cached, whole), (whole, whole + ROWS)]
            if not now:
                spots.pop(1)
            mixed = sum(
                jnp.dot(
                    r.astype(jnp.bfloat16),
                    values_ref[begin:end, :],
                    preferred_element_type=jnp.float32,
                )
                for r, (begin, end) in zip(raised, spots)
            )
            mixed = (mixed / total).astype(jnp.bfloat16)
            for h in range(heads):
                out_ref[h] = mixed[h * ROWS : (h + 1) * ROWS]


def attention(length, query, keys, values, head, heads, page_len):
    rows = query.shape[1]
    whole = pl.BlockSpec(keys.shape, lambda i: (0, 0))
    query = query[head : head + heads]
    block = pl.BlockSpec((heads, ROWS, HD), lambda i: (0, i, 0))
    return pl.pallas_call(
        functools.partial(attention_kernel, heads, page_len),
        grid=(rows // ROWS,),
        out_shape=jax.ShapeDtypeStruct((heads, rows, HD), jnp.bfloat16),
        in_specs=[pl.BlockSpec(memory_space=pltpu.SMEM), block, whole, whole],
        out_specs=block,
        compiler_params=pltpu.CompilerParams(vmem_limit_bytes=VMEM_LIMIT),
        cost_estimate=SLIGHT,
    )(length, query, keys, values)


def output_kernel(terms, onward, spots, *refs):
    refs = list(refs)
    place_ref = refs.pop(0)
    before = refs.pop(0) if onward else None
    blocks = [refs.pop(0) for _ in spots]
    weight, out_ref, left, right, total, left_sems, right_sems = refs
    member = place_ref[1]
    z, c = member // 2, member % 2
    local = right.shape[1] // 2
    rows = left.shape[1]
    copies = []
    for r, (shift, first, heads) in enumerate(terms):
        source = (z + SIDE - shift) % SIDE
        width = heads * HD
        mine = []
        for swapped in range(2):
            core = 1 - c if swapped else c
            for b in range(2):
                mine.append(
                    pltpu.make_async_copy(
                        weight.at[source * SIDE + 2 * b + core, :, pl.ds(first * HD, width)],
                        right.at[r, pl.ds(b * local, local), pl.ds(swapped * width, width)],
                        right_sems.at[r * 4 + swapped * 2 + b],
                    )
                )
        copies.append(mine)
    k = 0
    for ref, (swapped, parts) in zip(blocks, spots):
        for at, shift, head, row, count in parts:
            [r] = [r for r, (s, f, n) in enumerate(terms) if s == shift and f <= head < f + n]
            _, first, heads = terms[r]
            lane = (swapped * heads + head - first) * HD
            copies[r].append(
                pltpu.make_async_copy(
                    ref.at[pl.ds(at, count)],
                    left.at[r, pl.ds(row, count), pl.ds(lane, HD)],
                    left_sems.at[k],
                )
            )
            k += 1
    for mine in copies:
        for copy in mine:
            copy.start()
    for r, (_, _, heads) in enumerate(terms):
        for copy in copies[r]:
            copy.wait()
        for begin in range(0, rows, ROWS):
            part = lax.dot_general(
                left[r, begin : begin + ROWS, : 2 * heads * HD],
                right[r, :, : 2 * heads * HD],
                (((1,), (1,)), ((), ())),
                preferred_element_type=jnp.float32,
            )
            if r:
                part = part + total[begin : begin + ROWS, :]
            elif onward:
                part = part + before[begin : begin + ROWS, :]
            if r < len(terms) - 1:
                total[begin : begin + ROWS, :] = part
            else:
                out_ref[begin : begin + ROWS, :] = part.astype(out_ref.dtype)


def output_part(place, rows, terms, blocks, weight, last, before):
    onward = before is not None
    columns = 2 * weight.shape[1]
    most = max(heads for _, _, heads in terms) * 2 * HD
    spots = tuple(spot for _, spot in blocks)
    blocks = [block for block, _ in blocks]
    strips = sum(len(parts) for _, parts in spots)
    anywhere = pl.BlockSpec(memory_space=pl.ANY)
    vmem = pl.BlockSpec(memory_space=pltpu.VMEM)
    operands, in_specs = [place], [pl.BlockSpec(memory_space=pltpu.SMEM)]
    if onward:
        operands.append(before)
        in_specs.append(vmem)
    operands += [*blocks, weight]
    in_specs += [anywhere] * (len(blocks) + 1)
    return pl.pallas_call(
        functools.partial(output_kernel, terms, onward, spots),
        out_shape=jax.ShapeDtypeStruct((rows, columns), jnp.bfloat16 if last else jnp.float32),
        in_specs=in_specs,
        out_specs=vmem,
        scratch_shapes=[
            pltpu.VMEM((len(terms), rows, most), jnp.bfloat16),
            pltpu.VMEM((len(terms), columns, most), jnp.bfloat16),
            pltpu.VMEM((rows, columns), jnp.float32),
            pltpu.SemaphoreType.DMA((strips,)),
            pltpu.SemaphoreType.DMA((4 * len(terms),)),
        ],
        compiler_params=pltpu.CompilerParams(vmem_limit_bytes=VMEM_LIMIT),
        cost_estimate=SLIGHT,
    )(*operands)


def shards(
    tokens,
    norm_gain,
    w_query,
    b_query,
    keyvalue_weight,
    b_keyval,
    w_out,
    kv_pool,
    page_owner,
    page_index,
    prefix_pages,
    prompt_device,
):
    my_group = lax.axis_index("dp")
    my_member = lax.axis_index("mp")
    rows = tokens.shape[0]
    local, width_kv = keyvalue_weight.shape[0], keyvalue_weight.shape[2]
    page_len = kv_pool.shape[2]

    packed = jnp.concatenate([keyvalue_weight.reshape(local, 2 * width_kv), w_query], axis=1)
    ahead, behind, far = one_turn(packed, 0)
    outgoing = send_pages(
        my_group, page_owner, page_index, prefix_pages, prompt_device, kv_pool
    )
    arrived = lax.all_to_all(outgoing, "dp", split_axis=0, concat_axis=0)
    pages = arrived.reshape((-1,) + arrived.shape[2:])
    stack = jnp.concatenate([packed, ahead, *far, behind], axis=0)
    stack, _ = lax.optimization_barrier((stack, outgoing))
    stack, tokens, norm_gain, prompt_device = lax.optimization_barrier(
        (stack, tokens, norm_gain, prompt_device)
    )
    length = jnp.sum(jnp.where(prompt_device == my_group, prefix_pages, 0))
    owners = jnp.sum(jnp.where((prompt_device == my_group)[:, None], page_owner, 0), axis=0)
    slot = jnp.arange(owners.shape[0], dtype=jnp.int32)
    again = jnp.any((owners[:, None] == owners[None, :]) & (slot[None, :] < slot[:, None]), axis=1)
    slot_place = jnp.where(slot < length, owners * CAP + again, owners[0] * CAP).astype(jnp.int32)

    normed = rms_normed(tokens, norm_gain)
    positions = (length * page_len + jnp.arange(rows, dtype=jnp.int32)).astype(jnp.float32)
    frequency = rope_theta ** (-jnp.arange(HD // 2, dtype=jnp.float32) * 2.0 / HD)
    angles = positions[:, None] * frequency[None, :]
    cosine, sine = jnp.cos(angles), jnp.sin(angles)
    cosine = jnp.concatenate([cosine, cosine], axis=1)
    sine = jnp.concatenate([-sine, sine], axis=1)
    bias = jnp.concatenate([b_keyval.reshape(-1), b_query]).astype(jnp.float32)[None, :]
    ahead, behind, far = one_turn(stack, 1, (normed, cosine, sine, pages, slot_place, bias))
    ring_in = [
        (stack, 0, 0, 4),
        (ahead, 1, 0, 4),
        (behind, 3, 0, 4),
        (far[0], 2, 0, 2),
        (far[1], 2, 2, 2),
    ]

    ready, _ = lax.optimization_barrier((w_out.T, [ring_in[3][0], ring_in[4][0]]))
    moved = to_own_plane(ready)

    length = length.astype(jnp.int32)[None]
    place = jnp.stack([my_group, my_member]).astype(jnp.int32)
    query, keys, values = projection(
        slot_place, place, normed, ring_in, bias, cosine, sine, pages
    )

    moved, query = lax.optimization_barrier((moved, query))
    weight_out = lax.all_gather(moved, "dp", axis=0)

    spans = ((0, 2), (2, 3))
    sent = [
        attention(length, query, keys, values, head, count, page_len).reshape(count * rows, HD)
        for head, count in spans
    ]
    ahead = behind = None

    def strips(at, shift, head, begin, count):
        parts = []
        while count:
            row = begin % rows
            step = min(count, rows - row)
            parts.append((at, shift, head + begin // rows, row, step))
            at, begin, count = at + step, begin + step, count - step
        return parts

    held = []
    for k in range(len(sent) + 1):
        ups, downs, up_parts, down_parts = [], [], [], []
        if k < len(sent):
            head, size = spans[k][0], sent[k].shape[0]
            held.append((sent[k], {k: strips(0, 0, head, 0, size)}))
            ups, downs = [sent[k]], [sent[k]]
            up_parts = [(k, strips(0, 1, head, 0, size))]
            down_parts = [(k, strips(0, 3, head, 0, size))]
        if k:
            at = sent[k].shape[0] if k < len(sent) else 0
            head, size = spans[k - 1][0], sent[k - 1].shape[0]
            ups.append(ahead[: size // 2])
            downs.append(behind[size // 2 : size])
            up_parts.append((k - 1, strips(at, 2, head, 0, size // 2)))
            down_parts.append((k - 1, strips(at, 2, head, size // 2, size // 2)))
        ahead = shift_z(jnp.concatenate(ups, axis=0), 1)
        behind = shift_z(jnp.concatenate(downs, axis=0), 3)
        held += [(ahead, dict(up_parts)), (behind, dict(down_parts))]
    def both_cores(some):
        return [(array, parts, False) for array, parts in some] + [
            (swap_core(array), parts, True) for array, parts in some
        ]

    def strips_of(some):
        return [
            (array, (swapped, tuple(strip for strips in parts.values() for strip in strips)))
            for array, parts, swapped in some
        ]

    total, done, parts = None, 0, len(sent)
    for upto in (3 * (parts - 1), 3 * parts, len(held)):
        some = held[done:upto]
        if total is not None:
            arrays, total = lax.optimization_barrier(([array for array, _ in some], total))
            some = [(array, strips) for array, (_, strips) in zip(arrays, some)]
        found = sorted(
            {(strip[1], strip[2]) for _, by in some for strips in by.values() for strip in strips}
        )
        terms = []
        for shift in SHIFTS:
            heads = [head for at, head in found if at == shift]
            if heads:
                terms.append((shift, heads[0], len(heads)))
        total = output_part(
            place, rows, tuple(terms), strips_of(both_cores(some)), weight_out, upto == len(held), total
        )
        done = upto
    return total


def solution(mesh):
    return jax.shard_map(
        shards,
        mesh=mesh,
        in_specs=(
            P("dp", None),
            P(),
            P("dp", "mp"),
            P("mp"),
            P("dp", None, "mp"),
            P(None, "mp"),
            P("mp", "dp"),
            P(None, "dp", None, "mp"),
            P(),
            P(),
            P(),
            P(),
        ),
        out_specs=P("dp", "mp"),
        check_vma=False,
    )
```

```python
import functools

import jax
import jax.numpy as jnp
from jax import lax
from jax.experimental import pallas as pl
from jax.experimental.pallas import tpu as pltpu
from jax.sharding import PartitionSpec as P

HD = 128
CAP = 2
SIDE = 4
ROWS = 256
STEPS = 4
VMEM_LIMIT = 56 * 2**20
SLIGHT = pl.CostEstimate(flops=1, bytes_accessed=1, transcendentals=0)

rope_theta = 1000000.0
norm_eps = 1e-06
masked_score = -1e30

SHIFTS = (0, 1, 3, 2)


def rms_normed(rows, norm_gain):
    values = rows.astype(jnp.float32)
    inverse = lax.rsqrt(jnp.mean(values * values, axis=-1, keepdims=True) + norm_eps)
    return (values * inverse * norm_gain.astype(jnp.float32)).astype(jnp.bfloat16)


def shift_plane(block, d, turn):
    if d == 0:
        return block
    pairs = []
    for y in range(SIDE):
        for x in range(SIDE):
            for member in range(2 * SIDE):
                if member % 2 == turn:
                    target = y * SIDE + (x + d) % SIDE
                else:
                    target = (y + d) % SIDE * SIDE + x
                pairs.append(((y * SIDE + x) * 2 * SIDE + member, target * 2 * SIDE + member))
    return lax.ppermute(block, ("dp", "mp"), pairs)


def one_turn(block, turn, before_rest=None):
    half = block.shape[0] // 2
    ahead, behind = shift_plane(block, 1, turn), shift_plane(block, 3, turn)
    if before_rest is not None:
        ahead, behind, _ = lax.optimization_barrier((ahead, behind, before_rest))
    far = (shift_plane(ahead[:half], 1, turn), shift_plane(behind[half:], 3, turn))
    return ahead, behind, far


def ring_copies(pieces, layout, me, core, target, sems):
    x, y = me % SIDE, me // SIDE
    copies = []
    for ref, (outer, begin, count) in zip(pieces, layout):
        block = ref.shape[0] // count
        for i in range(count):
            inner = begin + i
            dx = inner + core * (outer - inner)
            dy = outer + core * (inner - outer)
            lane, width, place = target((x + SIDE - dx) % SIDE, (y + SIDE - dy) % SIDE)
            copies.append(
                pltpu.make_async_copy(
                    ref.at[pl.ds(i * block, block), pl.ds(lane, width)],
                    place,
                    sems.at[len(copies)],
                )
            )
    return copies


def shift_z(block, d):
    pairs = [(z * 2 + c, (z + d) % SIDE * 2 + c) for z in range(SIDE) for c in range(2)]
    return block if d == 0 else lax.ppermute(block, "mp", pairs)


def swap_core(block):
    return lax.ppermute(block, "mp", [(m, m ^ 1) for m in range(2 * SIDE)])


def to_own_plane(block):
    pairs = []
    for y in range(SIDE):
        for x in range(SIDE):
            for z in range(SIDE):
                for c in range(2):
                    source = (y * SIDE + x) * 8 + z * 2 + c
                    target = (z * SIDE + 2 * (x % 2) + c) * 8 + y * 2 + x // 2
                    pairs.append((source, target))
    return lax.ppermute(block, ("dp", "mp"), pairs)


def send_pages_kernel(pick_ref, device_ref, pool, out, sems):
    prompts = device_ref.shape[0]
    copies = [
        pltpu.make_async_copy(
            pool.at[:, pick_ref[p * CAP + r]], out.at[device_ref[p], r], sems.at[p * CAP + r]
        )
        for p in range(prompts)
        for r in range(CAP)
    ]
    for copy in copies:
        copy.start()
    for copy in copies:
        copy.wait()


def send_pages(my_group, page_owner, page_index, prefix_pages, prompt_device, kv_pool):
    prompts, slots = page_owner.shape
    _, held, page_len, width = kv_pool.shape
    slot = jnp.arange(slots, dtype=jnp.int32)[None, :]
    mine = (slot < prefix_pages[:, None]) & (page_owner == my_group)
    keyed = slot * held + page_index
    first = jnp.min(jnp.where(mine, keyed, slots * held), axis=1) % held
    final = jnp.max(jnp.where(mine, keyed, 0), axis=1) % held
    pick = jnp.stack([first, final], axis=1).reshape(-1)
    smem = pl.BlockSpec(memory_space=pltpu.SMEM)
    return pl.pallas_call(
        send_pages_kernel,
        out_shape=jax.ShapeDtypeStruct((prompts, CAP, 2, page_len, width), kv_pool.dtype),
        in_specs=[smem] * 2 + [pl.BlockSpec(memory_space=pl.ANY)],
        out_specs=pl.BlockSpec(memory_space=pltpu.VMEM),
        scratch_shapes=[pltpu.SemaphoreType.DMA((prompts * CAP,))],
    )(pick, prompt_device, kv_pool)


def projection_kernel(layout, place_ref, me_ref, normed_ref, bias_ref, cos_ref, sin_ref, pages, *refs):
    pieces, refs = refs[: len(layout)], refs[len(layout) :]
    query_ref, keys_ref, values_ref, weight_ref, weight_sems, page_sems = refs
    step = pl.program_id(0)
    slots = place_ref.shape[0]
    page_len = pages.shape[2]
    cached = slots * page_len

    local = weight_ref.shape[0] // (SIDE * SIDE)

    def target(x, y):
        row = pl.multiple_of((y * SIDE + x) * local, 16)
        return 0, weight_ref.shape[1], weight_ref.at[pl.ds(row, local)]

    weight_copies = ring_copies(pieces, layout, me_ref[0], me_ref[1] % 2, target, weight_sems)

    def page_copies():
        copies = []
        for j in range(slots):
            for part, held in ((0, keys_ref), (1, values_ref)):
                copies.append(
                    pltpu.make_async_copy(
                        pages.at[place_ref[j], part],
                        held.at[pl.ds(j * page_len, page_len)],
                        page_sems.at[j * 2 + part],
                    )
                )
        return copies

    @pl.when(step == 0)
    def _():
        for copy in weight_copies + page_copies():
            copy.start()
        for copy in weight_copies:
            copy.wait()

    cosine, sine = cos_ref[...], sin_ref[...]
    columns = weight_ref.shape[1]
    row = pl.multiple_of(cached + step * ROWS, ROWS)
    for begin in range(0, columns, 2 * HD):
        end = min(begin + 2 * HD, columns)
        projected = (
            jnp.dot(
                normed_ref[...], weight_ref[:, begin:end], preferred_element_type=jnp.float32
            )
            + bias_ref[:, begin:end]
        )
        for column in range(begin, end, HD):
            vector = projected[:, column - begin : column - begin + HD]
            if column == HD:
                values_ref[pl.ds(row, ROWS), :] = vector.astype(jnp.bfloat16)
                continue
            rotated = (vector * cosine + pltpu.roll(vector, HD // 2, 1) * sine).astype(jnp.bfloat16)
            if column == 0:
                keys_ref[pl.ds(row, ROWS), :] = rotated
            else:
                query_ref[column // HD - 2] = rotated

    @pl.when(step == pl.num_programs(0) - 1)
    def _():
        for copy in page_copies():
            copy.wait()


def projection(slot_place, me, normed, ring, bias, cosine, sine, pages):
    rows, depth = normed.shape
    columns = bias.shape[1]
    heads = columns // HD - 2
    slots, page_len = slot_place.shape[0], pages.shape[2]
    total = slots * page_len + rows
    smem = pl.BlockSpec(memory_space=pltpu.SMEM)
    anywhere = pl.BlockSpec(memory_space=pl.ANY)
    by_rows = pl.BlockSpec((ROWS, HD), lambda i: (i, 0))
    whole = pl.BlockSpec((total, HD), lambda i: (0, 0))
    return pl.pallas_call(
        functools.partial(projection_kernel, tuple(part[1:] for part in ring)),
        grid=(rows // ROWS,),
        out_shape=[
            jax.ShapeDtypeStruct((heads, rows, HD), jnp.bfloat16),
            jax.ShapeDtypeStruct((total, HD), jnp.bfloat16),
            jax.ShapeDtypeStruct((total, HD), jnp.bfloat16),
        ],
        in_specs=[
            smem,
            smem,
            pl.BlockSpec((ROWS, depth), lambda i: (i, 0)),
            pl.BlockSpec((1, columns), lambda i: (0, 0)),
            by_rows,
            by_rows,
            anywhere,
        ]
        + [anywhere] * len(ring),
        out_specs=[pl.BlockSpec((heads, ROWS, HD), lambda i: (0, i, 0)), whole, whole],
        scratch_shapes=[
            pltpu.VMEM((depth, columns), jnp.bfloat16),
            pltpu.SemaphoreType.DMA((SIDE * SIDE,)),
            pltpu.SemaphoreType.DMA((2 * slots,)),
        ],
        compiler_params=pltpu.CompilerParams(vmem_limit_bytes=VMEM_LIMIT),
        cost_estimate=SLIGHT,
    )(slot_place, me, normed, bias, cosine, sine, pages, *[part[0] for part in ring])


def attention_kernel(heads, page_len, length_ref, query_ref, keys_ref, values_ref, out_ref):
    step = pl.program_id(0)
    length = length_ref[0]
    cached = keys_ref.shape[0] - ROWS * STEPS
    query = query_ref[...].reshape(heads * ROWS, HD)
    to_exponent = HD ** (-0.5) * 1.4426950408889634

    def product(part):
        return lax.dot_general(
            query, part, (((1,), (1,)), ((), ())), preferred_element_type=jnp.float32
        )

    for now in range(STEPS):

        @pl.when(step == now)
        def _(now=now):
            whole = cached + now * ROWS
            live = lax.broadcasted_iota(jnp.int32, (1, cached), 1) < length * page_len
            scores = [jnp.where(live, product(keys_ref[0:cached, :]), masked_score)]
            if now:
                scores.append(product(keys_ref[cached:whole, :]))
            row_ids = lax.broadcasted_iota(jnp.int32, (ROWS, ROWS), 0)
            column_ids = lax.broadcasted_iota(jnp.int32, (ROWS, ROWS), 1)
            causal = jnp.concatenate([column_ids <= row_ids] * heads, axis=0)
            scores.append(
                jnp.where(causal, product(keys_ref[whole : whole + ROWS, :]), masked_score)
            )
            top = functools.reduce(
                jnp.maximum, [jnp.max(s, axis=-1, keepdims=True) for s in scores]
            )
            raised = [jnp.exp2((s - top) * to_exponent) for s in scores]
            total = sum(jnp.sum(r, axis=-1, keepdims=True) for r in raised)
            spots = [(0, cached), (cached, whole), (whole, whole + ROWS)]
            if not now:
                spots.pop(1)
            mixed = sum(
                jnp.dot(
                    r.astype(jnp.bfloat16),
                    values_ref[begin:end, :],
                    preferred_element_type=jnp.float32,
                )
                for r, (begin, end) in zip(raised, spots)
            )
            mixed = (mixed / total).astype(jnp.bfloat16)
            for h in range(heads):
                out_ref[h] = mixed[h * ROWS : (h + 1) * ROWS]


def attention(length, query, keys, values, head, heads, page_len):
    rows = query.shape[1]
    whole = pl.BlockSpec(keys.shape, lambda i: (0, 0))
    query = query[head : head + heads]
    block = pl.BlockSpec((heads, ROWS, HD), lambda i: (0, i, 0))
    return pl.pallas_call(
        functools.partial(attention_kernel, heads, page_len),
        grid=(rows // ROWS,),
        out_shape=jax.ShapeDtypeStruct((heads, rows, HD), jnp.bfloat16),
        in_specs=[pl.BlockSpec(memory_space=pltpu.SMEM), block, whole, whole],
        out_specs=block,
        compiler_params=pltpu.CompilerParams(vmem_limit_bytes=VMEM_LIMIT),
        cost_estimate=SLIGHT,
    )(length, query, keys, values)


def output_kernel(terms, onward, spots, *refs):
    refs = list(refs)
    place_ref = refs.pop(0)
    before = refs.pop(0) if onward else None
    blocks = [refs.pop(0) for _ in spots]
    weight, out_ref, left, right, total, left_sems, right_sems = refs
    member = place_ref[1]
    z, c = member // 2, member % 2
    local = right.shape[1] // 2
    rows = left.shape[1]
    copies = []
    for r, (shift, first, heads) in enumerate(terms):
        source = (z + SIDE - shift) % SIDE
        width = heads * HD
        mine = []
        for swapped in range(2):
            core = 1 - c if swapped else c
            for b in range(2):
                mine.append(
                    pltpu.make_async_copy(
                        weight.at[source * SIDE + 2 * b + core, :, pl.ds(first * HD, width)],
                        right.at[r, pl.ds(b * local, local), pl.ds(swapped * width, width)],
                        right_sems.at[r * 4 + swapped * 2 + b],
                    )
                )
        copies.append(mine)
    k = 0
    for ref, (swapped, parts) in zip(blocks, spots):
        for at, shift, head, row, count in parts:
            [r] = [r for r, (s, f, n) in enumerate(terms) if s == shift and f <= head < f + n]
            _, first, heads = terms[r]
            lane = (swapped * heads + head - first) * HD
            copies[r].append(
                pltpu.make_async_copy(
                    ref.at[pl.ds(at, count)],
                    left.at[r, pl.ds(row, count), pl.ds(lane, HD)],
                    left_sems.at[k],
                )
            )
            k += 1
    for mine in copies:
        for copy in mine:
            copy.start()
    for r, (_, _, heads) in enumerate(terms):
        for copy in copies[r]:
            copy.wait()
        for begin in range(0, rows, ROWS):
            part = lax.dot_general(
                left[r, begin : begin + ROWS, : 2 * heads * HD],
                right[r, :, : 2 * heads * HD],
                (((1,), (1,)), ((), ())),
                preferred_element_type=jnp.float32,
            )
            if r:
                part = part + total[begin : begin + ROWS, :]
            elif onward:
                part = part + before[begin : begin + ROWS, :]
            if r < len(terms) - 1:
                total[begin : begin + ROWS, :] = part
            else:
                out_ref[begin : begin + ROWS, :] = part.astype(out_ref.dtype)


def output_part(place, rows, terms, blocks, weight, last, before):
    onward = before is not None
    columns = 2 * weight.shape[1]
    most = max(heads for _, _, heads in terms) * 2 * HD
    spots = tuple(spot for _, spot in blocks)
    blocks = [block for block, _ in blocks]
    strips = sum(len(parts) for _, parts in spots)
    anywhere = pl.BlockSpec(memory_space=pl.ANY)
    vmem = pl.BlockSpec(memory_space=pltpu.VMEM)
    operands, in_specs = [place], [pl.BlockSpec(memory_space=pltpu.SMEM)]
    if onward:
        operands.append(before)
        in_specs.append(vmem)
    operands += [*blocks, weight]
    in_specs += [anywhere] * (len(blocks) + 1)
    return pl.pallas_call(
        functools.partial(output_kernel, terms, onward, spots),
        out_shape=jax.ShapeDtypeStruct((rows, columns), jnp.bfloat16 if last else jnp.float32),
        in_specs=in_specs,
        out_specs=vmem,
        scratch_shapes=[
            pltpu.VMEM((len(terms), rows, most), jnp.bfloat16),
            pltpu.VMEM((len(terms), columns, most), jnp.bfloat16),
            pltpu.VMEM((rows, columns), jnp.float32),
            pltpu.SemaphoreType.DMA((strips,)),
            pltpu.SemaphoreType.DMA((4 * len(terms),)),
        ],
        compiler_params=pltpu.CompilerParams(vmem_limit_bytes=VMEM_LIMIT),
        cost_estimate=SLIGHT,
    )(*operands)


def shards(
    tokens,
    norm_gain,
    w_query,
    b_query,
    keyvalue_weight,
    b_keyval,
    w_out,
    kv_pool,
    page_owner,
    page_index,
    prefix_pages,
    prompt_device,
):
    my_group = lax.axis_index("dp")
    my_member = lax.axis_index("mp")
    rows = tokens.shape[0]
    local, width_kv = keyvalue_weight.shape[0], keyvalue_weight.shape[2]
    page_len = kv_pool.shape[2]

    packed = jnp.concatenate([keyvalue_weight.reshape(local, 2 * width_kv), w_query], axis=1)
    ahead, behind, far = one_turn(packed, 0)
    outgoing = send_pages(
        my_group, page_owner, page_index, prefix_pages, prompt_device, kv_pool
    )
    arrived = lax.all_to_all(outgoing, "dp", split_axis=0, concat_axis=0)
    pages = arrived.reshape((-1,) + arrived.shape[2:])
    stack = jnp.concatenate([packed, ahead, *far, behind], axis=0)
    stack, _ = lax.optimization_barrier((stack, outgoing))
    stack, tokens, norm_gain, prompt_device = lax.optimization_barrier(
        (stack, tokens, norm_gain, prompt_device)
    )
    length = jnp.sum(jnp.where(prompt_device == my_group, prefix_pages, 0))
    owners = jnp.sum(jnp.where((prompt_device == my_group)[:, None], page_owner, 0), axis=0)
    slot = jnp.arange(owners.shape[0], dtype=jnp.int32)
    again = jnp.any((owners[:, None] == owners[None, :]) & (slot[None, :] < slot[:, None]), axis=1)
    slot_place = jnp.where(slot < length, owners * CAP + again, owners[0] * CAP).astype(jnp.int32)

    normed = rms_normed(tokens, norm_gain)
    positions = (length * page_len + jnp.arange(rows, dtype=jnp.int32)).astype(jnp.float32)
    frequency = rope_theta ** (-jnp.arange(HD // 2, dtype=jnp.float32) * 2.0 / HD)
    angles = positions[:, None] * frequency[None, :]
    cosine, sine = jnp.cos(angles), jnp.sin(angles)
    cosine = jnp.concatenate([cosine, cosine], axis=1)
    sine = jnp.concatenate([-sine, sine], axis=1)
    bias = jnp.concatenate([b_keyval.reshape(-1), b_query]).astype(jnp.float32)[None, :]
    ahead, behind, far = one_turn(stack, 1, (normed, cosine, sine, pages, slot_place, bias))
    ring_in = [
        (stack, 0, 0, 4),
        (ahead, 1, 0, 4),
        (behind, 3, 0, 4),
        (far[0], 2, 0, 2),
        (far[1], 2, 2, 2),
    ]

    ready, _ = lax.optimization_barrier((w_out.T, [ring_in[3][0], ring_in[4][0]]))
    moved = to_own_plane(ready)

    length = length.astype(jnp.int32)[None]
    place = jnp.stack([my_group, my_member]).astype(jnp.int32)
    query, keys, values = projection(
        slot_place, place, normed, ring_in, bias, cosine, sine, pages
    )

    moved, query = lax.optimization_barrier((moved, query))
    weight_out = lax.all_gather(moved, "dp", axis=0)

    spans = ((0, 3), (3, 2))
    sent = [
        attention(length, query, keys, values, head, count, page_len).reshape(count * rows, HD)
        for head, count in spans
    ]
    ahead = behind = None

    def strips(at, shift, head, begin, count):
        parts = []
        while count:
            row = begin % rows
            step = min(count, rows - row)
            parts.append((at, shift, head + begin // rows, row, step))
            at, begin, count = at + step, begin + step, count - step
        return parts

    held = []
    for k in range(len(sent) + 1):
        ups, downs, up_parts, down_parts = [], [], [], []
        if k < len(sent):
            head, size = spans[k][0], sent[k].shape[0]
            held.append((sent[k], {k: strips(0, 0, head, 0, size)}))
            ups, downs = [sent[k]], [sent[k]]
            up_parts = [(k, strips(0, 1, head, 0, size))]
            down_parts = [(k, strips(0, 3, head, 0, size))]
        if k:
            at = sent[k].shape[0] if k < len(sent) else 0
            head, size = spans[k - 1][0], sent[k - 1].shape[0]
            ups.append(ahead[: size // 2])
            downs.append(behind[size // 2 : size])
            up_parts.append((k - 1, strips(at, 2, head, 0, size // 2)))
            down_parts.append((k - 1, strips(at, 2, head, size // 2, size // 2)))
        ahead = shift_z(jnp.concatenate(ups, axis=0), 1)
        behind = shift_z(jnp.concatenate(downs, axis=0), 3)
        held += [(ahead, dict(up_parts)), (behind, dict(down_parts))]
    def both_cores(some):
        return [(array, parts, False) for array, parts in some] + [
            (swap_core(array), parts, True) for array, parts in some
        ]

    def strips_of(some):
        return [
            (array, (swapped, tuple(strip for strips in parts.values() for strip in strips)))
            for array, parts, swapped in some
        ]

    total, done, parts = None, 0, len(sent)
    for upto in (3 * parts, len(held)):
        some = held[done:upto]
        if total is not None:
            arrays, total = lax.optimization_barrier(([array for array, _ in some], total))
            some = [(array, strips) for array, (_, strips) in zip(arrays, some)]
        found = sorted(
            {(strip[1], strip[2]) for _, by in some for strips in by.values() for strip in strips}
        )
        terms = []
        for shift in SHIFTS:
            heads = [head for at, head in found if at == shift]
            if heads:
                terms.append((shift, heads[0], len(heads)))
        total = output_part(
            place, rows, tuple(terms), strips_of(both_cores(some)), weight_out, upto == len(held), total
        )
        done = upto
    return total


def solution(mesh):
    return jax.shard_map(
        shards,
        mesh=mesh,
        in_specs=(
            P("dp", None),
            P(),
            P("dp", "mp"),
            P("mp"),
            P("dp", None, "mp"),
            P(None, "mp"),
            P("mp", "dp"),
            P(None, "dp", None, "mp"),
            P(),
            P(),
            P(),
            P(),
        ),
        out_specs=P("dp", "mp"),
        check_vma=False,
    )
```
